256 devices in a mesh: section: 8 (over x, y_hi), fsdp: 32 (over y_lo, z, core).
Axes of the slice: x: 4, y: 4 (y_hi: 2, y_lo: 2; y = y_hi * 2 + y_lo), z: 8, core: 2. Of those that a mesh axis runs over, the one named last changes fastest.
Arguments:
- fwd_first: bfloat16 [8, 3584, 3072], P('section', 'fsdp'), may hold values from -6 to 6
- fwd_second: bfloat16 [8, 3584, 3072], P('section', 'fsdp'), may hold values from -6 to 6
- bwd_first: bfloat16 [8, 3584, 3072], P('section', 'fsdp'), may hold values from -6 to 6
- bwd_second: bfloat16 [8, 3584, 3072], P('section', 'fsdp'), may hold values from -6 to 6
- grad_first: bfloat16 [8, 3584, 3072], P('section', 'fsdp'), may hold values from -6 to 6
- grad_second: bfloat16 [8, 3584, 3072], P('section', 'fsdp'), may hold values from -6 to 6
- w_query: bfloat16 [8, 3072, 256], P('section', 'fsdp'), may hold values from -0.109375 to 0.109375
- w_key: bfloat16 [8, 3072, 256], P('section', 'fsdp'), may hold values from -0.109375 to 0.109375
- w_value: bfloat16 [8, 3072, 256], P('section', 'fsdp'), may hold values from -0.109375 to 0.109375
- w_out: bfloat16 [8, 256, 3072], P('section', None, 'fsdp'), may hold values from -0.375 to 0.375
Outputs:
- next_first: bfloat16 [8, 3584, 3072], P('section', 'fsdp')
- next_second: bfloat16 [8, 3584, 3072], P('section', 'fsdp')
- back_first: bfloat16 [8, 3584, 3072], P('section', 'fsdp')
- back_second: bfloat16 [8, 3584, 3072], P('section', 'fsdp')
- back_grad_first: bfloat16 [8, 3584, 3072], P('section', 'fsdp')
- back_grad_second: bfloat16 [8, 3584, 3072], P('section', 'fsdp')
- query_weight_grad: float32 [8, 3072, 256], P('section', 'fsdp')
- key_weight_grad: float32 [8, 3072, 256], P('section', 'fsdp')
- value_weight_grad: float32 [8, 3072, 256], P('section', 'fsdp')
- out_weight_grad: float32 [8, 256, 3072], P('section', None, 'fsdp')
The draws below stay inside these ranges and needn't reach their ends.
All inputs are finite; a program needn't handle non-finite values.
Results may differ from the reference program's by a relative error of at most 0.035.
Values may be sent and summed in bfloat16 or wider, within the bound.
No kernel may reach another device: no remote copies, remote signals or barrier semaphores. Data moves between devices by JAX's collectives and lax.ppermute only.
A program may use at most 128 MiB of HBM per device.

```python
import math
import jax
import jax.numpy as jnp
from jax import lax

D = 3072
HEADS = 2
HEAD_DIM = 128
TOK_DEV = 112
SEQ = 3584
N_SECTION = 8
N_FSDP = 32


def block_levels(own_key, dims, shards, smallest, top_value):
    def one(dim, blocks):
        steps = jax.random.uniform(jax.random.fold_in(jax.random.fold_in(own_key, 6), dim), (blocks,), jnp.float32, smallest / len(shards), top_value / len(shards))
        return jnp.repeat(jnp.exp(steps), dims[dim] // blocks).reshape((-1,) + (1,) * (len(dims) - dim - 1))

    factor_of = one(*shards[0])
    for cut in shards[1:]:
        factor_of = factor_of * one(*cut)
    return factor_of


def scatter_about(key, dims, deviation, bound, cuts=(), held_as=jnp.bfloat16):
    level = block_levels(key, dims, cuts, -0.22, 0.18) if cuts else 1.0
    entries = jax.random.normal(key, dims, jnp.float32) * deviation * level
    return jnp.minimum(jnp.maximum(entries, -bound), bound).astype(held_as)


def setup_inputs(seed: int = 0) -> dict:
    arg_keys = jax.random.split(jax.random.key(seed), 11)
    fwd_first = scatter_about(arg_keys[0], (N_SECTION, SEQ, D), 1.0, 6.0, ((0, 8), (1, 32)))
    fwd_second = scatter_about(arg_keys[1], (N_SECTION, SEQ, D), 1.0, 6.0, ((0, 8), (1, 32)))
    bwd_first = scatter_about(arg_keys[2], (N_SECTION, SEQ, D), 1.0, 6.0, ((0, 8), (1, 32)))
    bwd_second = scatter_about(arg_keys[3], (N_SECTION, SEQ, D), 1.0, 6.0, ((0, 8), (1, 32)))
    grad_first = scatter_about(arg_keys[4], (N_SECTION, SEQ, D), 1.0, 6.0, ((0, 8), (1, 32)))
    grad_second = scatter_about(arg_keys[5], (N_SECTION, SEQ, D), 1.0, 6.0, ((0, 8), (1, 32)))
    w_query = scatter_about(arg_keys[6], (N_SECTION, D, HEADS * HEAD_DIM), D ** -0.5, 0.109375, ((0, 8), (1, 32)))
    w_key = scatter_about(arg_keys[7], (N_SECTION, D, HEADS * HEAD_DIM), D ** -0.5, 0.109375, ((0, 8), (1, 32)))
    w_value = scatter_about(arg_keys[8], (N_SECTION, D, HEADS * HEAD_DIM), D ** -0.5, 0.109375, ((0, 8), (1, 32)))
    w_out = scatter_about(arg_keys[9], (N_SECTION, HEADS * HEAD_DIM, D), (HEADS * HEAD_DIM) ** -0.5, 0.375, ((0, 8), (2, 32)))
    return {"fwd_first": fwd_first, "fwd_second": fwd_second, "bwd_first": bwd_first, "bwd_second": bwd_second, "grad_first": grad_first, "grad_second": grad_second, "w_query": w_query, "w_key": w_key, "w_value": w_value, "w_out": w_out}


epsilon = 1e-05

def normalize(inputs):
    widened = inputs.astype(jnp.float32)
    inverse_rms = lax.rsqrt(lax.optimization_barrier(jnp.mean(widened * widened, axis=-1, keepdims=True)) + epsilon)
    return (widened * inverse_rms, inverse_rms)

def split_heads(matrix):
    return matrix.reshape(matrix.shape[0], HEADS, HEAD_DIM).astype(jnp.float32)

def merge_heads(tensor):
    return tensor.reshape(tensor.shape[0], HEADS * HEAD_DIM)

def project(inputs, w_query, w_key, w_value):
    normed, inverse_rms = normalize(inputs)
    normed_half = normed.astype(jnp.bfloat16)
    queries = jnp.dot(normed_half, w_query, preferred_element_type=jnp.float32).astype(jnp.bfloat16)
    keys_all = jnp.dot(normed_half, w_key, preferred_element_type=jnp.float32).astype(jnp.bfloat16)
    values_all = jnp.dot(normed_half, w_value, preferred_element_type=jnp.float32).astype(jnp.bfloat16)
    return (normed, inverse_rms, normed_half, queries, keys_all, values_all)

def attend(queries, keys_all, values_all):
    length = queries.shape[0]
    scores = jnp.einsum('qhd,khd->hqk', split_heads(queries), split_heads(keys_all)) / math.sqrt(HEAD_DIM)
    positions = jnp.arange(length, dtype=jnp.int32)
    causal_mask = positions[None, :] <= positions[:, None]
    masked = jnp.where(causal_mask[None], scores, -1e+30)
    highest = lax.optimization_barrier(jnp.max(masked, axis=-1, keepdims=True))
    weights_exp = jnp.where(causal_mask[None], jnp.exp(masked - highest), 0.0)
    row_total = lax.optimization_barrier(jnp.sum(weights_exp, axis=-1, keepdims=True))
    probs = weights_exp / row_total
    probs_half = probs.astype(jnp.bfloat16)
    attended = merge_heads(jnp.einsum('hqk,khd->qhd', probs_half.astype(jnp.float32), split_heads(values_all)))
    return (probs, probs_half, attended.astype(jnp.bfloat16))

def block_sum(left, right):
    left_blocks = left.reshape(N_FSDP, TOK_DEV, left.shape[1]).astype(jnp.float32)
    right_blocks = right.reshape(N_FSDP, TOK_DEV, right.shape[1]).astype(jnp.float32)
    partial_sums = jnp.einsum('btd,bte->bde', left_blocks, right_blocks).astype(jnp.bfloat16)
    partial_sums = lax.optimization_barrier(partial_sums)
    return lax.optimization_barrier(jnp.sum(partial_sums.astype(jnp.float32), axis=0))

def one_section(items):
    fwd_first, fwd_second, bwd_first, bwd_second, grad_first, grad_second, w_query, w_key, w_value, w_out = items
    scale = 1.0 / math.sqrt(HEAD_DIM)
    pieces = project(fwd_second, w_query, w_key, w_value)
    probs, probs_half, attended = attend(pieces[3], pieces[4], pieces[5])
    out_second = (fwd_first.astype(jnp.float32) + jnp.dot(attended, w_out, preferred_element_type=jnp.float32)).astype(jnp.bfloat16)
    normed, inverse_rms, normed_half, queries, keys_all, values_all = project(bwd_first, w_query, w_key, w_value)
    probs, probs_half, attended = attend(queries, keys_all, values_all)
    rec_first = (bwd_second.astype(jnp.float32) - jnp.dot(attended, w_out, preferred_element_type=jnp.float32)).astype(jnp.bfloat16)
    attended_grad = jnp.dot(grad_second, w_out.T, preferred_element_type=jnp.float32).astype(jnp.bfloat16)
    prob_grad = jnp.einsum('qhd,khd->hqk', split_heads(attended_grad), split_heads(values_all))
    row_dot = lax.optimization_barrier(jnp.sum(probs * prob_grad, axis=-1, keepdims=True))
    score_grad = (probs * (prob_grad - row_dot) * scale).astype(jnp.bfloat16).astype(jnp.float32)
    query_grad = merge_heads(jnp.einsum('hqk,khd->qhd', score_grad, split_heads(keys_all))).astype(jnp.bfloat16)
    key_grad = merge_heads(jnp.einsum('hqk,qhd->khd', score_grad, split_heads(queries))).astype(jnp.bfloat16)
    value_grad = merge_heads(jnp.einsum('hqk,qhd->khd', probs_half.astype(jnp.float32), split_heads(attended_grad))).astype(jnp.bfloat16)
    normed_grad = jnp.dot(query_grad, w_query.T, preferred_element_type=jnp.float32)
    normed_grad = normed_grad + jnp.dot(key_grad, w_key.T, preferred_element_type=jnp.float32)
    normed_grad = normed_grad + jnp.dot(value_grad, w_value.T, preferred_element_type=jnp.float32)
    input_grad = inverse_rms * (normed_grad - normed * lax.optimization_barrier(jnp.mean(normed_grad * normed, axis=-1, keepdims=True)))
    cot_second = (grad_first.astype(jnp.float32) + input_grad).astype(jnp.bfloat16)
    query_wgrad = block_sum(normed_half, query_grad)
    key_wgrad = block_sum(normed_half, key_grad)
    value_wgrad = block_sum(normed_half, value_grad)
    out_wgrad = block_sum(attended, grad_second)
    return (fwd_second, out_second, rec_first, bwd_first, grad_second, cot_second, query_wgrad, key_wgrad, value_wgrad, out_wgrad)

def shift_down(stacked):
    return jnp.concatenate([jnp.zeros_like(stacked[:1]), stacked[:-1]], axis=0)

def shift_up(stacked):
    return jnp.concatenate([stacked[1:], jnp.zeros_like(stacked[:1])], axis=0)

def reference(fwd_first, fwd_second, bwd_first, bwd_second, grad_first, grad_second, w_query, w_key, w_value, w_out):
    results = lax.map(one_section, (fwd_first, fwd_second, bwd_first, bwd_second, grad_first, grad_second, w_query, w_key, w_value, w_out))
    out_first, out_second, rec_first, rec_second, cot_first, cot_second, query_wgrad, key_wgrad, value_wgrad, out_wgrad = results
    return (shift_down(out_first), shift_down(out_second), shift_up(rec_first), shift_up(rec_second), shift_up(cot_first), shift_up(cot_second), query_wgrad, key_wgrad, value_wgrad, out_wgrad)
```

```python
import math

import jax
import jax.numpy as jnp
from jax import lax
from jax.sharding import Mesh
from jax.sharding import PartitionSpec as P

HEADS = 2
HEAD_DIM = 128
Y, Z, C = 2, 8, 2
NEG = -1e30
SCALE = 1.0 / math.sqrt(HEAD_DIM)
F32 = jnp.float32
BF16 = jnp.bfloat16

epsilon = 1e-05


def passed_along(value, steps):
    count = lax.axis_size("section")
    first, last = (max(0, -steps), min(count, count - steps))
    return lax.ppermute(
        value, "section", [(source, source + steps) for source in range(first, last)]
    )


def swap(value, axis):
    return lax.ppermute(value, axis, [(0, 1), (1, 0)])


def ring(value, step):
    return lax.ppermute(value, "z", [(i, (i + step) % Z) for i in range(Z)])


def ring_gather(block):
    half = block.shape[0] // 2
    blocks = {0: block}
    ahead = behind = block
    for distance in range(1, Z // 2):
        ahead, behind = ring(ahead, -1), ring(behind, 1)
        blocks[distance], blocks[-distance] = ahead, behind
    blocks[Z // 2] = jnp.concatenate([ring(ahead[:half], -1), ring(behind[half:], 1)], axis=0)
    return blocks


def ring_reduce(parts):
    half = parts[0].shape[0] // 2
    far = parts[Z // 2].astype(BF16)
    ahead = ring(far[:half], 1).astype(F32)
    behind = ring(far[half:], -1).astype(F32)
    last = Z // 2 - 1
    ahead = jnp.concatenate([parts[last][:half] + ahead, parts[last][half:]], axis=0)
    behind = jnp.concatenate([parts[-last][:half], parts[-last][half:] + behind], axis=0)
    for distance in range(last, 0, -1):
        ahead = ring(ahead.astype(BF16), 1).astype(F32)
        behind = ring(behind.astype(BF16), -1).astype(F32)
        if distance > 1:
            ahead = ahead + parts[distance - 1]
            behind = behind + parts[1 - distance]
    return parts[0].astype(F32) + ahead + behind


def normalize(inputs):
    widened = inputs.astype(F32)
    inverse_rms = lax.rsqrt(jnp.mean(widened * widened, axis=-1, keepdims=True) + epsilon)
    return (widened * inverse_rms, inverse_rms)


def dot(left, right, left_dim=1, right_dim=0):
    return lax.dot_general(
        left, right, (((left_dim,), (right_dim,)), ((), ())), preferred_element_type=F32
    )


def chip_positions(y, z, c, tokens):
    spot = jnp.arange(tokens, dtype=jnp.int32)
    base = (y * Z + z) * (C * tokens)
    return jnp.concatenate([base + c * tokens + spot, base + (1 - c) * tokens + spot])


def placed_rows(blocks, z):
    rows, columns = blocks[0].shape[1:]
    whole = jnp.zeros((Y, Z, rows, columns), BF16)
    for distance, block in blocks.items():
        whole = lax.dynamic_update_slice(whole, block[:, None], (0, (z + distance) % Z, 0, 0))
    return whole.reshape(Y * Z * rows, columns)


def owner_parts(gradient, z):
    rows = gradient.shape[0] // (Y * Z)
    split = gradient.reshape(Y, Z, rows, gradient.shape[1])
    return {
        distance: lax.dynamic_slice(
            split, (0, (z + distance) % Z, 0, 0), (Y, 1, rows, gradient.shape[1])
        )[:, 0]
        for distance in range(1 - Z // 2, Z // 2 + 1)
    }


def attend(queries, keys, values, mask):
    scores = jnp.where(mask, dot(queries, keys, 1, 1) * SCALE, NEG)
    highest = jnp.max(scores, axis=-1, keepdims=True)
    weights = jnp.where(mask, jnp.exp(scores - highest), 0.0)
    total = jnp.sum(weights, axis=-1, keepdims=True)
    return weights, highest, total


def merged(highest, total, other_highest, other_total):
    top = jnp.maximum(highest, other_highest)
    own = jnp.exp(highest - top)
    other = jnp.exp(other_highest - top)
    whole = total * own + other_total * other
    safe = jnp.where(whole > 0.0, whole, 1.0)
    return own / safe, other / safe


def per_device(
    fwd_first,
    fwd_second,
    bwd_first,
    bwd_second,
    grad_first,
    grad_second,
    w_query,
    w_key,
    w_value,
    w_out,
):
    c, y, z = lax.axis_index("c"), lax.axis_index("yl"), lax.axis_index("z")
    tokens = fwd_first.shape[1]
    chip = C * tokens
    stream_f, stream_b, cot_out = fwd_second[0], bwd_first[0], grad_second[0]

    out_rows = w_out[0].T
    by_head = [
        jnp.concatenate(
            [
                part[:, head * HEAD_DIM : (head + 1) * HEAD_DIM]
                for part in (w_key[0], w_value[0], w_query[0], out_rows)
            ],
            axis=1,
        )
        for head in range(HEADS)
    ]
    mine = jnp.where(c == 0, by_head[0], by_head[1])
    given = jnp.where(c == 0, by_head[1], by_head[0])
    got = swap(given, "c")
    block = jnp.where(
        c == 0, jnp.concatenate([mine, got], axis=0), jnp.concatenate([got, mine], axis=0)
    )
    other_block = swap(block, "yl")
    pair = jnp.where(y == 0, jnp.stack([block, other_block]), jnp.stack([other_block, block]))
    wide = 2 * HEAD_DIM
    w_kv = placed_rows(ring_gather(pair[:, :, :wide]), z)
    w_qo = placed_rows(ring_gather(pair[:, :, wide:]), z)
    w_q, w_o = w_qo[:, :HEAD_DIM], w_qo[:, HEAD_DIM:]

    next_first = passed_along(stream_f, 1)
    back_second = passed_along(stream_b, -1)
    back_grad_first = passed_along(cot_out, -1)

    both_b = jnp.concatenate([stream_b, swap(stream_b, "c")], axis=0)
    both_f = jnp.concatenate([stream_f, swap(stream_f, "c")], axis=0)
    both_g = jnp.concatenate([cot_out, swap(cot_out, "c")], axis=0)
    normed_b, inverse_rms = normalize(both_b)
    normed_own, inverse_own = normed_b[:tokens], inverse_rms[:tokens]
    half_b = normed_b.astype(BF16)
    half_f = normalize(both_f)[0].astype(BF16)

    kv_b = dot(half_b, w_kv).astype(BF16)
    q_b = dot(half_b, w_q).astype(BF16)
    da_b = dot(both_g, w_o).astype(BF16)
    kv_f = dot(half_f, w_kv).astype(BF16)
    q_f = dot(half_f, w_q).astype(BF16)

    w_kv_other, w_qo_other = swap(w_kv, "c"), swap(w_qo, "c")
    w_q_other, w_o_other = w_qo_other[:, :HEAD_DIM], w_qo_other[:, HEAD_DIM:]

    def lend(value):
        return lax.ppermute(value, "yl", [(1, 0)])

    def give_back(value):
        return lax.ppermute(value, "yl", [(0, 1)])

    order = [0] + [d for k in range(1, Z // 2) for d in (k, -k)] + [Z // 2]
    key_index = jnp.concatenate([chip_positions(y, (z + d) % Z, c, tokens) for d in order])
    query_index = jnp.concatenate(
        [chip_positions(y, z, c, tokens), chip_positions(1 - y, z, c, tokens)]
    )
    mask = key_index[None, :] <= query_index[:, None]

    lent_b = lend(jnp.concatenate([q_b, da_b], axis=1))
    queries_b = jnp.concatenate([q_b, lent_b[:, :HEAD_DIM]], axis=0)
    grads_b = jnp.concatenate([da_b, lent_b[:, HEAD_DIM:]], axis=0)
    blocks = ring_gather(kv_b)
    kv = jnp.concatenate([blocks[d] for d in order], axis=0)
    keys_b, values_b = kv[:, :HEAD_DIM], kv[:, HEAD_DIM:]

    lent_f = lend(q_f)
    queries_f = jnp.concatenate([q_f, lent_f], axis=0)
    blocks = ring_gather(kv_f)
    kv = jnp.concatenate([blocks[d] for d in order], axis=0)
    keys_f, values_f = kv[:, :HEAD_DIM], kv[:, HEAD_DIM:]

    def exchanged(columns):
        stats = jnp.concatenate(columns, axis=1)
        sent = jnp.where(y == 0, stats[chip:], stats[:chip])
        received = swap(sent, "yl")
        none = jnp.concatenate(
            [jnp.full((chip, 1), NEG, F32), jnp.zeros((chip, len(columns) - 1), F32)], axis=1
        )
        full = jnp.where(
            y == 0,
            jnp.concatenate([none, received], axis=0),
            jnp.concatenate([received, none], axis=0),
        )
        return [full[:, k : k + 1] for k in range(len(columns))]

    def finish(weights, values, own_scale):
        partial = dot(weights.astype(BF16), values) * own_scale
        return partial[:chip] + give_back(partial[chip:].astype(BF16)).astype(F32)

    weights, highest, total = attend(queries_b, keys_b, mask=mask, values=values_b)
    prob_grad = dot(grads_b, values_b, 1, 1)
    row_part = jnp.sum(weights * prob_grad, axis=-1, keepdims=True)
    other_highest, other_total, other_row = exchanged([highest, total, row_part])
    own_scale, other_scale = merged(highest, total, other_highest, other_total)
    row_dot = row_part * own_scale + other_row * other_scale
    probs = weights * own_scale
    score_grad = (probs * (prob_grad - row_dot) * SCALE).astype(BF16)
    probs_half = probs.astype(BF16)
    kv_part = jnp.concatenate(
        [dot(score_grad, queries_b, 0, 0), dot(probs_half, grads_b, 0, 0)], axis=1
    )
    kv_grad = ring_reduce(
        {d: kv_part[i * chip : (i + 1) * chip] for i, d in enumerate(order)}
    ).astype(BF16)
    q_part = dot(score_grad, keys_b)
    q_grad = (q_part[:chip] + give_back(q_part[chip:].astype(BF16)).astype(F32)).astype(BF16)
    attended_part = dot(probs_half, values_b)
    attended_b = (
        attended_part[:chip] + give_back(attended_part[chip:].astype(BF16)).astype(F32)
    ).astype(BF16)
    attended_other = swap(attended_b[tokens:], "c")
    rec_first = (
        bwd_second[0].astype(F32)
        - dot(attended_b[:tokens], w_o, 1, 1)
        - dot(attended_other, w_o_other, 1, 1)
    ).astype(BF16)
    back_first = passed_along(rec_first, -1)

    weights, highest, total = attend(queries_f, keys_f, mask=mask, values=values_f)
    other_highest, other_total = exchanged([highest, total])
    own_scale, _ = merged(highest, total, other_highest, other_total)
    attended_f = finish(weights, values_f, own_scale).astype(BF16)
    attended_other = swap(attended_f[tokens:], "c")
    updated = (
        fwd_first[0].astype(F32)
        + dot(attended_f[:tokens], w_o, 1, 1)
        + dot(attended_other, w_o_other, 1, 1)
    ).astype(BF16)
    next_second = passed_along(updated, 1)

    grads = jnp.concatenate([kv_grad, q_grad], axis=1)
    grads_other = swap(grads[tokens:], "c")
    normed_grad = (
        dot(grads[:tokens, :wide], w_kv, 1, 1)
        + dot(grads[:tokens, wide:], w_q, 1, 1)
        + dot(grads_other[:, :wide], w_kv_other, 1, 1)
        + dot(grads_other[:, wide:], w_q_other, 1, 1)
    )
    input_grad = inverse_own * (
        normed_grad - normed_own * jnp.mean(normed_grad * normed_own, axis=-1, keepdims=True)
    )
    cot_second = (grad_first[0].astype(F32) + input_grad).astype(BF16)
    back_grad_second = passed_along(cot_second, -1)

    qo_wpart = jnp.concatenate(
        [dot(half_b, q_grad, 0, 0), dot(both_g, attended_b, 0, 0)], axis=1
    ).astype(BF16)
    kv_wpart = dot(half_b, kv_grad, 0, 0).astype(BF16)

    def summed(part):
        over_z = ring_reduce(owner_parts(part, z))
        sent = jnp.where(y == 0, over_z[1], over_z[0]).astype(BF16)
        return jnp.where(y == 0, over_z[0], over_z[1]) + swap(sent, "yl").astype(F32)

    whole = jnp.concatenate([summed(kv_wpart), summed(qo_wpart)], axis=1)
    rows = whole.shape[0] // C
    own = jnp.where(c == 0, whole[:rows], whole[rows:])
    other = swap(jnp.where(c == 0, whole[rows:], whole[:rows]), "c")

    def heads_of(index):
        span = slice(index * HEAD_DIM, (index + 1) * HEAD_DIM)
        return jnp.where(
            c == 0,
            jnp.concatenate([own[:, span], other[:, span]], axis=1),
            jnp.concatenate([other[:, span], own[:, span]], axis=1),
        )

    return (
        next_first[None],
        next_second[None],
        back_first[None],
        back_second[None],
        back_grad_first[None],
        back_grad_second[None],
        heads_of(2)[None],
        heads_of(0)[None],
        heads_of(1)[None],
        heads_of(3).T[None],
    )


def solution(mesh):
    sections = mesh.devices.shape[0]
    split = Mesh(mesh.devices.reshape(sections, Y, Z, C), ("section", "yl", "z", "c"))
    fsdp = ("yl", "z", "c")
    rows = P("section", fsdp, None)
    columns = P("section", None, fsdp)
    return jax.shard_map(
        per_device,
        mesh=split,
        in_specs=(rows,) * 9 + (columns,),
        out_specs=(rows,) * 9 + (columns,),
        check_vma=False,
    )
```

```python
import math

import jax
import jax.numpy as jnp
import numpy as np
from jax import lax
from jax.sharding import Mesh
from jax.sharding import PartitionSpec as P

HEADS = 2
HEAD_DIM = 128
Y, Z, C = 2, 8, 2
NEG = -1e30
SCALE = 1.0 / math.sqrt(HEAD_DIM)
F32 = jnp.float32
BF16 = jnp.bfloat16

epsilon = 1e-05


def passed_along(value, steps):
    count = lax.axis_size("section")
    first, last = (max(0, -steps), min(count, count - steps))
    return lax.ppermute(
        value, "section", [(source, source + steps) for source in range(first, last)]
    )


def swap(value, axis):
    return lax.ppermute(value, axis, [(0, 1), (1, 0)])


def ring(value, step):
    return lax.ppermute(value, "z", [(i, (i + step) % Z) for i in range(Z)])


def ring_gather(block, beside):
    beside = dict(beside)
    half = block.shape[0] // 2
    blocks = {0: block}
    ahead = behind = block
    for distance in range(1, Z // 2 + 1):
        if distance in beside:
            ahead, behind, beside[distance] = lax.optimization_barrier(
                (ahead, behind, beside[distance])
            )
        if distance == Z // 2:
            break
        ahead, behind = ring(ahead, -1), ring(behind, 1)
        blocks[distance], blocks[-distance] = ahead, behind
    blocks[Z // 2] = jnp.concatenate([ring(ahead[:half], -1), ring(behind[half:], 1)], axis=0)
    return blocks, beside


def ring_reduce(parts, beside):
    beside = dict(beside)
    half = parts[0].shape[0] // 2
    far = parts[Z // 2].astype(BF16)
    ahead = ring(far[:half], 1).astype(F32)
    behind = ring(far[half:], -1).astype(F32)
    last = Z // 2 - 1
    ahead = jnp.concatenate([parts[last][:half] + ahead, parts[last][half:]], axis=0)
    behind = jnp.concatenate([parts[-last][:half], parts[-last][half:] + behind], axis=0)
    for distance in range(last, 0, -1):
        if distance in beside:
            ahead, behind, beside[distance] = lax.optimization_barrier(
                (ahead, behind, beside[distance])
            )
        ahead = ring(ahead.astype(BF16), 1).astype(F32)
        behind = ring(behind.astype(BF16), -1).astype(F32)
        if distance > 1:
            ahead = ahead + parts[distance - 1]
            behind = behind + parts[1 - distance]
    return parts[0].astype(F32) + ahead + behind, beside


def inverse_rms(inputs):
    widened = inputs.astype(F32)
    return lax.rsqrt(jnp.mean(widened * widened, axis=-1, keepdims=True) + epsilon)


def dot(left, right, left_dim=1, right_dim=0):
    return lax.dot_general(
        left, right, (((left_dim,), (right_dim,)), ((), ())), preferred_element_type=F32
    )


def placed_rows(blocks, z):
    rows, columns = blocks[0].shape[1:]
    whole = jnp.zeros((Y, Z, rows, columns), BF16)
    for distance, block in blocks.items():
        whole = lax.dynamic_update_slice(whole, block[:, None], (0, (z + distance) % Z, 0, 0))
    return whole.reshape(Y * Z * rows, columns)


def owner_parts(gradient, z):
    rows = gradient.shape[0] // (Y * Z)
    split = gradient.reshape(Y, Z, rows, gradient.shape[1])
    return {
        distance: lax.dynamic_slice(
            split, (0, (z + distance) % Z, 0, 0), (Y, 1, rows, gradient.shape[1])
        )[:, 0]
        for distance in range(1 - Z // 2, Z // 2 + 1)
    }


def attend(queries, keys, mask):
    scores = jnp.where(mask, dot(queries, keys, 1, 1) * SCALE, NEG)
    highest = jnp.max(scores, axis=-1, keepdims=True)
    weights = jnp.where(mask, jnp.exp(scores - highest), 0.0)
    total = jnp.sum(weights, axis=-1, keepdims=True)
    return weights, highest, total


def merged(highest, total, other_highest, other_total):
    top = jnp.maximum(highest, other_highest)
    own = jnp.exp(highest - top)
    other = jnp.exp(other_highest - top)
    whole = total * own + other_total * other
    safe = jnp.where(whole > 0.0, whole, 1.0)
    return own / safe, other / safe


def per_device(
    fwd_first,
    fwd_second,
    bwd_first,
    bwd_second,
    grad_first,
    grad_second,
    w_query,
    w_key,
    w_value,
    w_out,
):
    c, y, z = lax.axis_index("c"), lax.axis_index("yl"), lax.axis_index("z")
    tokens = fwd_first.shape[1]
    chip = C * tokens
    stream_f, stream_b, cot_out = fwd_second[0], bwd_first[0], grad_second[0]

    wide = 2 * HEAD_DIM
    out_rows = w_out[0].T

    def by_core(own, other):
        return jnp.where(
            c == 0,
            jnp.concatenate([own, other], axis=0),
            jnp.concatenate([other, own], axis=0),
        )

    by_head = [
        jnp.concatenate(
            [
                part[:, head * HEAD_DIM : (head + 1) * HEAD_DIM]
                for part in (w_key[0], w_value[0], w_query[0], out_rows)
            ],
            axis=1,
        )
        for head in range(HEADS)
    ]
    mine = jnp.where(c == 0, by_head[0], by_head[1])
    given = jnp.where(c == 0, by_head[1], by_head[0])
    block = by_core(mine, swap(given, "c"))
    other_block = by_core(
        swap(mine, "yl"),
        lax.ppermute(given, ("yl", "c"), [(i, Y * C - 1 - i) for i in range(Y * C)]),
    )
    pair = jnp.where(y == 0, jnp.stack([block, other_block]), jnp.stack([other_block, block]))

    streams = jnp.concatenate([stream_f, stream_b, cot_out], axis=0)
    streams_other = swap(streams, "c")
    pair, early_f, early_bg = lax.optimization_barrier((pair, stream_f, streams[tokens:]))
    next_first = passed_along(early_f, 1)
    back_both = passed_along(early_bg, -1)

    both_f, both_b, both_g = (
        jnp.concatenate([own, streams_other[k * tokens : (k + 1) * tokens]], axis=0)
        for k, own in enumerate((stream_f, stream_b, cot_out))
    )
    inverse_b, inverse_f = inverse_rms(both_b), inverse_rms(both_f)
    half_b = (both_b.astype(F32) * inverse_b).astype(BF16)
    half_f = (both_f.astype(F32) * inverse_f).astype(BF16)

    w_qo = lax.all_gather(pair[:, :, wide:], "z", axis=1).reshape(-1, wide)
    w_q, w_o = w_qo[:, :HEAD_DIM], w_qo[:, HEAD_DIM:]
    weight_blocks, beside = ring_gather(pair[:, :, :wide], {4: (half_b, half_f, both_g)})
    half_b, half_f, both_g = beside[4]
    w_kv = placed_rows(weight_blocks, z)

    kv_own = jnp.concatenate(
        [dot(half_b, w_kv).astype(BF16), dot(half_f, w_kv).astype(BF16)], axis=1
    )
    q_b = dot(half_b, w_q).astype(BF16)
    da_b = dot(both_g, w_o).astype(BF16)
    q_f = dot(half_f, w_q).astype(BF16)

    def heads_together(own, other):
        return jnp.where(
            c == 0,
            jnp.concatenate([own, other], axis=1),
            jnp.concatenate([other, own], axis=1),
        )

    def over_heads(function, *rows):
        sent = function(*(part[tokens:] for part in rows)).astype(BF16)
        return function(*(part[:tokens] for part in rows)) + swap(sent, "c").astype(F32)

    section = lax.axis_index("section")

    def after_first(value):
        return jnp.where(section > 0, value, jnp.zeros_like(value))[None]

    def before_last(value):
        return jnp.where(
            section < lax.axis_size("section") - 1, value, jnp.zeros_like(value)
        )[None]

    def lend(value):
        return lax.ppermute(value, "yl", [(1, 0)])

    def give_back(value):
        return lax.ppermute(value, "yl", [(0, 1)])

    order = [0] + [d for k in range(1, Z // 2) for d in (k, -k)] + [Z // 2]
    spot = jnp.arange(Z * chip, dtype=jnp.int32)
    inside = spot % chip
    inside = jnp.where(
        inside < tokens, inside + c * tokens, inside + (1 - c) * tokens - tokens
    )
    distances = jnp.asarray(np.repeat(np.array(order, np.int32), chip))
    key_index = ((y * Z + (z + distances) % Z) * chip + inside).astype(jnp.int32)
    spot = jnp.arange(2 * chip, dtype=jnp.int32)
    inside = spot % chip
    inside = jnp.where(
        inside < tokens, inside + c * tokens, inside + (1 - c) * tokens - tokens
    )
    query_index = (jnp.where(spot < chip, y, 1 - y) * Z + z) * chip + inside
    mask = key_index[None, :] <= query_index[:, None]

    lent = lend(jnp.concatenate([q_b, da_b, q_f], axis=1))
    queries_b, grads_b, queries_f = (
        jnp.concatenate([own, lent[:, k * HEAD_DIM : (k + 1) * HEAD_DIM]], axis=0)
        for k, own in enumerate((q_b, da_b, q_f))
    )
    blocks, beside = ring_gather(
        kv_own, {3: (next_first, back_both), 4: (queries_b, grads_b, queries_f)}
    )
    next_first, back_both = beside[3]
    queries_b, grads_b, queries_f = beside[4]
    kv = jnp.concatenate([blocks[d] for d in order], axis=0)
    keys_b, values_b, keys_f, values_f = (
        kv[:, k * HEAD_DIM : (k + 1) * HEAD_DIM] for k in range(4)
    )

    def exchanged(columns):
        stats = jnp.concatenate(columns, axis=1)
        sent = jnp.where(y == 0, stats[chip:], stats[:chip])
        received = swap(sent, "yl")
        none = jnp.concatenate(
            [jnp.full((chip, 1), NEG, F32), jnp.zeros((chip, len(columns) - 1), F32)], axis=1
        )
        full = jnp.where(
            y == 0,
            jnp.concatenate([none, received], axis=0),
            jnp.concatenate([received, none], axis=0),
        )
        return [full[:, k : k + 1] for k in range(len(columns))]

    weights, highest, total = attend(queries_b, keys_b, mask)
    weights_f, highest_f, total_f = attend(queries_f, keys_f, mask)
    prob_grad = dot(grads_b, values_b, 1, 1)
    row_part = jnp.sum(weights * prob_grad, axis=-1, keepdims=True)
    other_highest, other_total, other_row, other_highest_f, other_total_f = exchanged(
        [highest, total, row_part, highest_f, total_f]
    )
    own_scale, other_scale = merged(highest, total, other_highest, other_total)
    own_scale_f, _ = merged(highest_f, total_f, other_highest_f, other_total_f)
    row_dot = row_part * own_scale + other_row * other_scale
    probs = weights * own_scale
    score_grad = (probs * (prob_grad - row_dot) * SCALE).astype(BF16)
    probs_half = probs.astype(BF16)
    kv_part = jnp.concatenate(
        [dot(score_grad, queries_b, 0, 0), dot(probs_half, grads_b, 0, 0)], axis=1
    )
    shared = jnp.concatenate(
        [
            dot(score_grad, keys_b),
            dot(probs_half, values_b),
            dot(weights_f.astype(BF16), values_f) * own_scale_f,
        ],
        axis=1,
    )
    rows_own = shared[:chip] + give_back(shared[chip:].astype(BF16)).astype(F32)
    q_grad, attended_b, attended_f = (
        rows_own[:, k * HEAD_DIM : (k + 1) * HEAD_DIM].astype(BF16) for k in range(3)
    )
    zeros = jnp.zeros_like(q_grad)
    qo_wpart = dot(
        jnp.concatenate([half_b, both_g], axis=0),
        jnp.concatenate(
            [
                jnp.concatenate([q_grad, zeros], axis=1),
                jnp.concatenate([zeros, attended_b], axis=1),
            ],
            axis=0,
        ),
        0,
        0,
    ).astype(BF16)
    by_chip = qo_wpart.reshape(Y, Z, -1, wide).transpose(1, 0, 2, 3)
    qo_sum = lax.psum_scatter(by_chip, "z", scatter_dimension=0, tiled=False)

    change_b, change_f = over_heads(
        lambda *rows: jnp.stack([dot(row, w_o, 1, 1) for row in rows], axis=0),
        attended_b,
        attended_f,
    )
    rec_first = (bwd_second[0].astype(F32) - change_b).astype(BF16)
    updated = (fwd_first[0].astype(F32) + change_f).astype(BF16)
    kv_grad, beside = ring_reduce(
        {d: kv_part[i * chip : (i + 1) * chip] for i, d in enumerate(order)},
        {1: (rec_first, updated)},
    )
    kv_grad = kv_grad.astype(BF16)
    rec_first, updated = beside[1]
    back_first = passed_along(rec_first, -1)
    next_second = passed_along(updated, 1)

    normed_grad = over_heads(
        lambda kv_rows, q_rows: dot(kv_rows, w_kv, 1, 1) + dot(q_rows, w_q, 1, 1),
        kv_grad,
        q_grad,
    )
    normed_own, inverse_own = stream_b.astype(F32) * inverse_b[:tokens], inverse_b[:tokens]
    input_grad = inverse_own * (
        normed_grad - normed_own * jnp.mean(normed_grad * normed_own, axis=-1, keepdims=True)
    )
    cot_second = (grad_first[0].astype(F32) + input_grad).astype(BF16)

    kv_wpart = dot(half_b, kv_grad, 0, 0).astype(BF16)

    over_z, beside = ring_reduce(
        owner_parts(kv_wpart, z),
        {
            3: (back_first,),
            2: (
                cot_second,
                next_second,
                before_last(back_both[:tokens]),
                before_last(back_both[tokens:]),
            ),
            1: (after_first(next_first),),
        },
    )
    (back_first,), (next_first,) = beside[3], beside[1]
    cot_second, next_second, back_second, back_grad_first = beside[2]
    back_grad_second = passed_along(cot_second, -1)
    over_z, back_grad_second, qo_sum, back_first, next_second = lax.optimization_barrier(
        (over_z, back_grad_second, qo_sum, before_last(back_first), after_first(next_second))
    )
    rows = over_z.shape[1] // C
    corner = jnp.concatenate([over_z, qo_sum.astype(F32)], axis=2).reshape(Y, C, rows, 2 * wide)

    def of(y_, c_):
        return lax.dynamic_slice(corner, (y_, c_, 0, 0), (1, 1, rows, 2 * wide))[0, 0]

    def of_other(c_):
        return of(1 - y, c_).astype(BF16)

    across = lax.ppermute(
        of_other(1 - c), ("yl", "c"), [(i, Y * C - 1 - i) for i in range(Y * C)]
    ).astype(F32)
    own = of(y, c) + swap(of_other(c), "yl").astype(F32)
    other = swap(of(y, 1 - c).astype(BF16), "c").astype(F32) + across

    def heads_of(index):
        span = slice(index * HEAD_DIM, (index + 1) * HEAD_DIM)
        return heads_together(own[:, span], other[:, span])

    return (
        next_first,
        next_second,
        back_first,
        back_second,
        back_grad_first,
        before_last(back_grad_second),
        heads_of(2)[None],
        heads_of(0)[None],
        heads_of(1)[None],
        heads_of(3).T[None],
    )


def solution(mesh):
    sections = mesh.devices.shape[0]
    split = Mesh(mesh.devices.reshape(sections, Y, Z, C), ("section", "yl", "z", "c"))
    fsdp = ("yl", "z", "c")
    rows = P("section", fsdp, None)
    columns = P("section", None, fsdp)
    return jax.shard_map(
        per_device,
        mesh=split,
        in_specs=(rows,) * 9 + (columns,),
        out_specs=(rows,) * 9 + (columns,),
        check_vma=False,
    )
```

```python
import functools
import math

import jax
import jax.numpy as jnp
import numpy as np
from jax import lax
from jax.experimental import pallas as pl
from jax.experimental.pallas import tpu as pltpu
from jax.sharding import Mesh
from jax.sharding import PartitionSpec as P

HEADS = 2
HEAD_DIM = 128
Y, Z, C = 2, 8, 2
NEG = -1e30
SCALE = 1.0 / math.sqrt(HEAD_DIM)
F32 = jnp.float32
BF16 = jnp.bfloat16

epsilon = 1e-05


def passed_along(value, steps):
    count = lax.axis_size("section")
    first, last = (max(0, -steps), min(count, count - steps))
    return lax.ppermute(
        value, "section", [(source, source + steps) for source in range(first, last)]
    )


def swap(value, axis):
    return lax.ppermute(value, axis, [(0, 1), (1, 0)])


def ring(value, step):
    return lax.ppermute(value, "z", [(i, (i + step) % Z) for i in range(Z)])


def ring_gather(block, beside):
    beside = dict(beside)
    half = block.shape[0] // 2
    blocks = {0: block}
    ahead = behind = block
    for distance in range(1, Z // 2 + 1):
        if distance in beside:
            ahead, behind, beside[distance] = lax.optimization_barrier(
                (ahead, behind, beside[distance])
            )
        if distance == Z // 2:
            break
        ahead, behind = ring(ahead, -1), ring(behind, 1)
        blocks[distance], blocks[-distance] = ahead, behind
    blocks[Z // 2] = jnp.concatenate([ring(ahead[:half], -1), ring(behind[half:], 1)], axis=0)
    return blocks, beside


def ring_reduce(parts, beside):
    beside = dict(beside)
    half = parts[0].shape[0] // 2
    far = parts[Z // 2].astype(BF16)
    ahead = ring(far[:half], 1).astype(F32)
    behind = ring(far[half:], -1).astype(F32)
    last = Z // 2 - 1
    ahead = jnp.concatenate([parts[last][:half] + ahead, parts[last][half:]], axis=0)
    behind = jnp.concatenate([parts[-last][:half], parts[-last][half:] + behind], axis=0)
    for distance in range(last, 0, -1):
        if distance in beside:
            ahead, behind, beside[distance] = lax.optimization_barrier(
                (ahead, behind, beside[distance])
            )
        ahead = ring(ahead.astype(BF16), 1).astype(F32)
        behind = ring(behind.astype(BF16), -1).astype(F32)
        if distance > 1:
            ahead = ahead + parts[distance - 1]
            behind = behind + parts[1 - distance]
    return parts[0].astype(F32) + ahead + behind, beside


def inverse_rms(inputs):
    widened = inputs.astype(F32)
    return lax.rsqrt(jnp.mean(widened * widened, axis=-1, keepdims=True) + epsilon)


def dot(left, right, left_dim=1, right_dim=0):
    return lax.dot_general(
        left, right, (((left_dim,), (right_dim,)), ((), ())), preferred_element_type=F32
    )


def softmax_parts(scores, mask):
    scores = jnp.where(mask, scores, NEG)
    highest = jnp.max(scores, axis=-1, keepdims=True)
    weights = jnp.where(mask, jnp.exp(scores - highest), 0.0)
    return weights, highest, jnp.sum(weights, axis=-1, keepdims=True)


def statistics_kernel(chunk, q_b, g_b, q_f, kv, query_at, key_at, stats, out_f):
    def step(index, carry):
        rows = pl.ds(pl.multiple_of(index * chunk, chunk), chunk)
        mask = key_at[...] <= query_at[rows, :]
        weights, highest, total = softmax_parts(
            dot(q_b[rows, :], kv[:, :HEAD_DIM], 1, 1) * SCALE, mask
        )
        prob_grad = dot(g_b[rows, :], kv[:, HEAD_DIM : 2 * HEAD_DIM], 1, 1)
        stats[rows, 0:1] = highest
        stats[rows, 1:2] = total
        stats[rows, 2:3] = jnp.sum(weights * prob_grad, axis=-1, keepdims=True)
        weights, highest, total = softmax_parts(
            dot(q_f[rows, :], kv[:, 2 * HEAD_DIM : 3 * HEAD_DIM], 1, 1) * SCALE, mask
        )
        stats[rows, 3:4] = highest
        stats[rows, 4:5] = total
        out_f[rows, :] = dot(weights.astype(BF16), kv[:, 3 * HEAD_DIM :])
        return carry

    lax.fori_loop(0, q_b.shape[0] // chunk, step, 0)


def gradients_kernel(chunk, q_b, g_b, kv, query_at, key_at, scales, out_rows, out_kv):
    out_kv[...] = jnp.zeros_like(out_kv)

    def step(index, carry):
        rows = pl.ds(pl.multiple_of(index * chunk, chunk), chunk)
        mask = key_at[...] <= query_at[rows, :]
        queries, grads = q_b[rows, :], g_b[rows, :]
        keys, values = kv[:, :HEAD_DIM], kv[:, HEAD_DIM : 2 * HEAD_DIM]
        scores = jnp.where(mask, dot(queries, keys, 1, 1) * SCALE, NEG)
        probs = jnp.where(mask, jnp.exp(scores - scales[rows, 0:1]), 0.0) * scales[rows, 1:2]
        prob_grad = dot(grads, values, 1, 1)
        score_grad = (probs * (prob_grad - scales[rows, 2:3]) * SCALE).astype(BF16)
        probs_half = probs.astype(BF16)
        out_rows[rows, :HEAD_DIM] = dot(score_grad, keys)
        out_rows[rows, HEAD_DIM:] = dot(probs_half, values)
        out_kv[:, :HEAD_DIM] += dot(score_grad, queries, 0, 0)
        out_kv[:, HEAD_DIM:] += dot(probs_half, grads, 0, 0)
        return carry

    lax.fori_loop(0, q_b.shape[0] // chunk, step, 0)


def kernel_call(kernel, chunk, outs, products, exps, operands):
    rows, keys = operands[0].shape[0], Z * operands[0].shape[0] // 2
    return pl.pallas_call(
        functools.partial(kernel, chunk),
        out_shape=[jax.ShapeDtypeStruct(shape, F32) for shape in outs],
        compiler_params=pltpu.CompilerParams(vmem_limit_bytes=32 * 1024 * 1024),
        cost_estimate=pl.CostEstimate(
            flops=2 * products * rows * keys * HEAD_DIM,
            bytes_accessed=sum(operand.size * operand.dtype.itemsize for operand in operands),
            transcendentals=exps * rows * keys,
        ),
    )(*operands)


def merged(highest, total, other_highest, other_total):
    top = jnp.maximum(highest, other_highest)
    own = jnp.exp(highest - top)
    other = jnp.exp(other_highest - top)
    whole = total * own + other_total * other
    inverse = 1.0 / jnp.where(whole > 0.0, whole, 1.0)
    return top, inverse, own * inverse, other * inverse


def per_device(
    fwd_first,
    fwd_second,
    bwd_first,
    bwd_second,
    grad_first,
    grad_second,
    w_query,
    w_key,
    w_value,
    w_out,
):
    c, y, z = lax.axis_index("c"), lax.axis_index("yl"), lax.axis_index("z")
    tokens = fwd_first.shape[1]
    chip = C * tokens
    stream_f, stream_b, cot_out = fwd_second[0], bwd_first[0], grad_second[0]

    wide = 2 * HEAD_DIM
    out_rows = w_out[0].T

    def by_core(own, other):
        return jnp.where(
            c == 0,
            jnp.concatenate([own, other], axis=0),
            jnp.concatenate([other, own], axis=0),
        )

    by_head = [
        jnp.concatenate(
            [
                part[:, head * HEAD_DIM : (head + 1) * HEAD_DIM]
                for part in (w_key[0], w_value[0], w_query[0], out_rows)
            ],
            axis=1,
        )
        for head in range(HEADS)
    ]
    mine = jnp.where(c == 0, by_head[0], by_head[1])
    given_away = jnp.where(c == 0, by_head[1], by_head[0])
    mine, given_away, stream_f, stream_b, cot_out = lax.optimization_barrier(
        (mine, given_away, stream_f, stream_b, cot_out)
    )
    block = by_core(mine, swap(given_away, "c"))
    other_block = by_core(
        swap(mine, "yl"),
        lax.ppermute(given_away, ("yl", "c"), [(i, Y * C - 1 - i) for i in range(Y * C)]),
    )
    pair = jnp.where(y == 0, jnp.stack([block, other_block]), jnp.stack([other_block, block]))

    stream_bg = jnp.concatenate([stream_b, cot_out], axis=0)
    other_f, other_bg = swap(stream_f, "c"), swap(stream_bg, "c")
    pair, early_f, early_bg = lax.optimization_barrier((pair, stream_f, stream_bg))
    next_first = passed_along(early_f, 1)
    back_both = passed_along(early_bg, -1)

    both_f = jnp.concatenate([stream_f, other_f], axis=0)
    both_b = jnp.concatenate([stream_b, other_bg[:tokens]], axis=0)
    both_g = jnp.concatenate([cot_out, other_bg[tokens:]], axis=0)
    inverse_b, inverse_f = inverse_rms(both_b), inverse_rms(both_f)
    half_b = (both_b.astype(F32) * inverse_b).astype(BF16)
    half_f = (both_f.astype(F32) * inverse_f).astype(BF16)

    w_kvqo = lax.all_gather(pair, "z", axis=1).reshape(-1, 2 * wide)
    w_kvq, w_o = w_kvqo[:, : 3 * HEAD_DIM], w_kvqo[:, 3 * HEAD_DIM :]

    half = jnp.concatenate([half_b, half_f], axis=0)
    kv_all = dot(half, w_kvqo[:, :wide]).astype(BF16)
    kv_own = jnp.concatenate([kv_all[:chip], kv_all[chip:]], axis=1)

    def heads_together(own, other):
        return jnp.where(
            c == 0,
            jnp.concatenate([own, other], axis=1),
            jnp.concatenate([other, own], axis=1),
        )

    section = lax.axis_index("section")

    def after_first(value):
        return jnp.where(section > 0, value, jnp.zeros_like(value))[None]

    def before_last(value):
        return jnp.where(
            section < lax.axis_size("section") - 1, value, jnp.zeros_like(value)
        )[None]

    def lend(value):
        return lax.ppermute(value, "yl", [(1, 0)])

    def give_back(value):
        return lax.ppermute(value, "yl", [(0, 1)])

    order = [0] + [d for k in range(1, Z // 2) for d in (k, -k)] + [Z // 2]
    spot = jnp.arange(Z * chip, dtype=jnp.int32)
    inside = spot % chip
    inside = jnp.where(
        inside < tokens, inside + c * tokens, inside + (1 - c) * tokens - tokens
    )
    distances = jnp.asarray(np.repeat(np.array(order, np.int32), chip))
    key_index = ((y * Z + (z + distances) % Z) * chip + inside).astype(jnp.int32)
    spot = jnp.arange(2 * chip, dtype=jnp.int32)
    inside = spot % chip
    inside = jnp.where(
        inside < tokens, inside + c * tokens, inside + (1 - c) * tokens - tokens
    )
    query_index = (jnp.where(spot < chip, y, 1 - y) * Z + z) * chip + inside
    key_at, query_at = key_index[None, :], query_index[:, None]

    blocks, beside = ring_gather(
        kv_own, {2: (half, both_g), 4: (next_first, back_both)}
    )
    half_late, both_g_late = beside[2]
    next_first, back_both = beside[4]
    q_all = dot(half_late, w_kvqo[:, wide : 3 * HEAD_DIM]).astype(BF16)
    q_b, q_f = q_all[:chip], q_all[chip:]
    da_b = dot(both_g_late, w_o).astype(BF16)
    lent = lend(jnp.concatenate([q_b, da_b, q_f], axis=1))
    blocks[Z // 2], lent = lax.optimization_barrier((blocks[Z // 2], lent))
    queries_b, grads_b, queries_f = (
        jnp.concatenate([own, lent[:, k * HEAD_DIM : (k + 1) * HEAD_DIM]], axis=0)
        for k, own in enumerate((q_b, da_b, q_f))
    )
    kv = jnp.concatenate([blocks[d] for d in order], axis=0)
    def exchanged(columns):
        stats = jnp.concatenate(columns, axis=1)
        sent = jnp.where(y == 0, stats[chip:], stats[:chip])
        received = swap(sent, "yl")
        none = jnp.concatenate(
            [jnp.full((chip, 1), NEG, F32), jnp.zeros((chip, len(columns) - 1), F32)], axis=1
        )
        full = jnp.where(
            y == 0,
            jnp.concatenate([none, received], axis=0),
            jnp.concatenate([received, none], axis=0),
        )
        return [full[:, k : k + 1] for k in range(len(columns))]

    stats, out_f = kernel_call(
        statistics_kernel,
        tokens,
        [(2 * chip, 8), (2 * chip, HEAD_DIM)],
        4,
        2,
        (queries_b, grads_b, queries_f, kv, query_at, key_at),
    )
    highest, total, row_part, highest_f, total_f = (stats[:, k : k + 1] for k in range(5))
    other_highest, other_total, other_row, other_highest_f, other_total_f = exchanged(
        [highest, total, row_part, highest_f, total_f]
    )
    top, inverse, own_scale, other_scale = merged(highest, total, other_highest, other_total)
    own_scale_f = merged(highest_f, total_f, other_highest_f, other_total_f)[2]
    row_dot = row_part * own_scale + other_row * other_scale
    rows_b, kv_part = kernel_call(
        gradients_kernel,
        tokens,
        [(2 * chip, wide), (Z * chip, wide)],
        6,
        1,
        (
            queries_b,
            grads_b,
            kv,
            query_at,
            key_at,
            jnp.concatenate([top, inverse, row_dot], axis=1),
        ),
    )
    def given(rows):
        return rows[:chip] + give_back(rows[chip:].astype(BF16)).astype(F32)

    def projected(attended, received):
        return dot(attended[:tokens], w_o, 1, 1) + received.astype(F32)

    def for_other_core(attended):
        return swap(dot(attended[tokens:], w_o, 1, 1).astype(BF16), "c")

    attended_f = given(out_f * own_scale_f).astype(BF16)
    received_f = for_other_core(attended_f)
    updated = (fwd_first[0].astype(F32) + projected(attended_f, received_f)).astype(BF16)

    next_second = passed_along(updated, 1)

    own_rows = given(rows_b)
    q_grad, attended_b = own_rows[:, :HEAD_DIM].astype(BF16), own_rows[:, HEAD_DIM:].astype(BF16)
    received_b = for_other_core(attended_b)
    rec_first = (bwd_second[0].astype(F32) - projected(attended_b, received_b)).astype(BF16)

    kv_grad, beside = ring_reduce(
        {d: kv_part[i * chip : (i + 1) * chip] for i, d in enumerate(order)},
        {1: (rec_first,)},
    )
    (rec_first,) = beside[1]
    kv_grad = kv_grad.astype(BF16)
    back_first = passed_along(rec_first, -1)

    grads = jnp.concatenate([kv_grad, q_grad], axis=1)
    grads_late, next_second = lax.optimization_barrier((grads, next_second))
    received = swap(dot(grads_late[tokens:], w_kvq, 1, 1).astype(BF16), "c")
    normed_grad = dot(grads_late[:tokens], w_kvq, 1, 1) + received.astype(F32)
    normed_own, inverse_own = stream_b.astype(F32) * inverse_b[:tokens], inverse_b[:tokens]
    input_grad = inverse_own * (
        normed_grad - normed_own * jnp.mean(normed_grad * normed_own, axis=-1, keepdims=True)
    )
    cot_second = (grad_first[0].astype(F32) + input_grad).astype(BF16)

    zeros = jnp.zeros_like(q_grad)
    wpart = dot(
        jnp.concatenate([half_b, both_g], axis=0),
        jnp.concatenate(
            [
                jnp.concatenate([grads, zeros], axis=1),
                jnp.concatenate([zeros, zeros, zeros, attended_b], axis=1),
            ],
            axis=0,
        ),
        0,
        0,
    ).astype(BF16)
    by_chip = wpart.reshape(Y, Z, -1, 2 * wide).transpose(1, 0, 2, 3)
    over_z = lax.psum_scatter(
        by_chip.reshape(-1, 2 * wide), "z", scatter_dimension=0, tiled=True
    )
    cot_second, next_first, back_both = lax.optimization_barrier(
        (cot_second, next_first, back_both)
    )
    back_grad_second = passed_along(cot_second, -1)
    next_first = after_first(next_first)
    back_second, back_grad_first = before_last(back_both[:tokens]), before_last(back_both[tokens:])
    over_z, next_first, back_second, back_grad_first, next_second, back_first, back_grad_second = (
        lax.optimization_barrier(
            (
                over_z,
                next_first,
                back_second,
                back_grad_first,
                next_second,
                back_first,
                back_grad_second,
            )
        )
    )
    rows = over_z.shape[0] // (Y * C)
    corner = over_z.astype(F32).reshape(Y, C, rows, 2 * wide)

    def of(y_, c_):
        return lax.dynamic_slice(corner, (y_, c_, 0, 0), (1, 1, rows, 2 * wide))[0, 0]

    def of_other(c_):
        return of(1 - y, c_).astype(BF16)

    across = lax.ppermute(
        of_other(1 - c), ("yl", "c"), [(i, Y * C - 1 - i) for i in range(Y * C)]
    ).astype(F32)
    own = of(y, c) + swap(of_other(c), "yl").astype(F32)
    other = swap(of(y, 1 - c).astype(BF16), "c").astype(F32) + across

    def heads_of(index):
        span = slice(index * HEAD_DIM, (index + 1) * HEAD_DIM)
        return heads_together(own[:, span], other[:, span])

    return (
        next_first,
        after_first(next_second),
        before_last(back_first),
        back_second,
        back_grad_first,
        before_last(back_grad_second),
        heads_of(2)[None],
        heads_of(0)[None],
        heads_of(1)[None],
        heads_of(3).T[None],
    )


def solution(mesh):
    sections = mesh.devices.shape[0]
    split = Mesh(mesh.devices.reshape(sections, Y, Z, C), ("section", "yl", "z", "c"))
    fsdp = ("yl", "z", "c")
    rows = P("section", fsdp, None)
    columns = P("section", None, fsdp)
    return jax.shard_map(
        per_device,
        mesh=split,
        in_specs=(rows,) * 9 + (columns,),
        out_specs=(rows,) * 9 + (columns,),
        check_vma=False,
    )
```

```python
import functools
import math

import jax
import jax.numpy as jnp
import numpy as np
from jax import lax
from jax.experimental import pallas as pl
from jax.experimental.pallas import tpu as pltpu
from jax.sharding import Mesh
from jax.sharding import PartitionSpec as P

HEADS = 2
HEAD_DIM = 128
Y, Z, C = 2, 8, 2
NEG = -1e30
SCALE = 1.0 / math.sqrt(HEAD_DIM)
F32 = jnp.float32
BF16 = jnp.bfloat16

epsilon = 1e-05


def passed_along(value, steps):
    count = lax.axis_size("section")
    first, last = (max(0, -steps), min(count, count - steps))
    return lax.ppermute(
        value, "section", [(source, source + steps) for source in range(first, last)]
    )


def swap(value, axis):
    return lax.ppermute(value, axis, [(0, 1), (1, 0)])


def ring(value, step):
    return lax.ppermute(value, "z", [(i, (i + step) % Z) for i in range(Z)])


def ring_gather(block, beside):
    beside = dict(beside)
    half = block.shape[0] // 2
    blocks = {0: block}
    ahead = behind = block
    for distance in range(1, Z // 2 + 1):
        if distance in beside:
            ahead, behind, beside[distance] = lax.optimization_barrier(
                (ahead, behind, beside[distance])
            )
        if distance == Z // 2:
            break
        ahead, behind = ring(ahead, -1), ring(behind, 1)
        blocks[distance], blocks[-distance] = ahead, behind
    blocks[Z // 2] = jnp.concatenate([ring(ahead[:half], -1), ring(behind[half:], 1)], axis=0)
    return blocks, beside


def ring_reduce(parts, beside):
    beside = dict(beside)
    half = parts[0].shape[0] // 2
    far = parts[Z // 2].astype(BF16)
    ahead = ring(far[:half], 1).astype(F32)
    behind = ring(far[half:], -1).astype(F32)
    last = Z // 2 - 1
    ahead = jnp.concatenate([parts[last][:half] + ahead, parts[last][half:]], axis=0)
    behind = jnp.concatenate([parts[-last][:half], parts[-last][half:] + behind], axis=0)
    for distance in range(last, 0, -1):
        if distance in beside:
            ahead, behind, beside[distance] = lax.optimization_barrier(
                (ahead, behind, beside[distance])
            )
        ahead = ring(ahead.astype(BF16), 1).astype(F32)
        behind = ring(behind.astype(BF16), -1).astype(F32)
        if distance > 1:
            ahead = ahead + parts[distance - 1]
            behind = behind + parts[1 - distance]
    return parts[0].astype(F32) + ahead + behind, beside


def inverse_rms(inputs):
    widened = inputs.astype(F32)
    return lax.rsqrt(jnp.mean(widened * widened, axis=-1, keepdims=True) + epsilon)


def dot(left, right, left_dim=1, right_dim=0):
    return lax.dot_general(
        left, right, (((left_dim,), (right_dim,)), ((), ())), preferred_element_type=F32
    )


def softmax_parts(scores, mask):
    scores = jnp.where(mask, scores, NEG)
    highest = jnp.max(scores, axis=-1, keepdims=True)
    weights = jnp.where(mask, jnp.exp(scores - highest), 0.0)
    return weights, highest, jnp.sum(weights, axis=-1, keepdims=True)


def statistics_kernel(chunk, q_b, g_b, q_f, kv, query_at, key_at, stats, out_f):
    def step(index, carry):
        rows = pl.ds(pl.multiple_of(index * chunk, chunk), chunk)
        mask = key_at[...] <= query_at[rows, :]
        weights, highest, total = softmax_parts(
            dot(q_b[rows, :], kv[:, :HEAD_DIM], 1, 1) * SCALE, mask
        )
        prob_grad = dot(g_b[rows, :], kv[:, HEAD_DIM : 2 * HEAD_DIM], 1, 1)
        stats[rows, 0:1] = highest
        stats[rows, 1:2] = total
        stats[rows, 2:3] = jnp.sum(weights * prob_grad, axis=-1, keepdims=True)
        weights, highest, total = softmax_parts(
            dot(q_f[rows, :], kv[:, 2 * HEAD_DIM : 3 * HEAD_DIM], 1, 1) * SCALE, mask
        )
        stats[rows, 3:4] = highest
        stats[rows, 4:5] = total
        out_f[rows, :] = dot(weights.astype(BF16), kv[:, 3 * HEAD_DIM :])
        return carry

    lax.fori_loop(0, q_b.shape[0] // chunk, step, 0)


def gradients_kernel(chunk, q_b, g_b, kv, query_at, key_at, scales, out_rows, out_kv):
    out_kv[...] = jnp.zeros_like(out_kv)

    def step(index, carry):
        rows = pl.ds(pl.multiple_of(index * chunk, chunk), chunk)
        mask = key_at[...] <= query_at[rows, :]
        queries, grads = q_b[rows, :], g_b[rows, :]
        keys, values = kv[:, :HEAD_DIM], kv[:, HEAD_DIM : 2 * HEAD_DIM]
        scores = jnp.where(mask, dot(queries, keys, 1, 1) * SCALE, NEG)
        probs = jnp.where(mask, jnp.exp(scores - scales[rows, 0:1]), 0.0) * scales[rows, 1:2]
        prob_grad = dot(grads, values, 1, 1)
        score_grad = (probs * (prob_grad - scales[rows, 2:3]) * SCALE).astype(BF16)
        probs_half = probs.astype(BF16)
        out_rows[rows, :HEAD_DIM] = dot(score_grad, keys)
        out_rows[rows, HEAD_DIM:] = dot(probs_half, values)
        out_kv[:, :HEAD_DIM] += dot(score_grad, queries, 0, 0)
        out_kv[:, HEAD_DIM:] += dot(probs_half, grads, 0, 0)
        return carry

    lax.fori_loop(0, q_b.shape[0] // chunk, step, 0)


def kernel_call(kernel, chunk, outs, products, exps, operands):
    rows, keys = operands[0].shape[0], Z * operands[0].shape[0] // 2
    return pl.pallas_call(
        functools.partial(kernel, chunk),
        out_shape=[jax.ShapeDtypeStruct(shape, F32) for shape in outs],
        compiler_params=pltpu.CompilerParams(vmem_limit_bytes=32 * 1024 * 1024),
        cost_estimate=pl.CostEstimate(
            flops=2 * products * rows * keys * HEAD_DIM,
            bytes_accessed=sum(operand.size * operand.dtype.itemsize for operand in operands),
            transcendentals=exps * rows * keys,
        ),
    )(*operands)


def merged(highest, total, other_highest, other_total):
    top = jnp.maximum(highest, other_highest)
    own = jnp.exp(highest - top)
    other = jnp.exp(other_highest - top)
    whole = total * own + other_total * other
    inverse = 1.0 / jnp.where(whole > 0.0, whole, 1.0)
    return top, inverse, own * inverse, other * inverse


def per_device(
    fwd_first,
    fwd_second,
    bwd_first,
    bwd_second,
    grad_first,
    grad_second,
    w_query,
    w_key,
    w_value,
    w_out,
):
    c, y, z = lax.axis_index("c"), lax.axis_index("yl"), lax.axis_index("z")
    tokens = fwd_first.shape[1]
    chip = C * tokens
    stream_f, stream_b, cot_out = fwd_second[0], bwd_first[0], grad_second[0]

    wide = 2 * HEAD_DIM
    out_rows = w_out[0].T

    def by_core(own, other):
        return jnp.where(
            c == 0,
            jnp.concatenate([own, other], axis=0),
            jnp.concatenate([other, own], axis=0),
        )

    by_head = [
        jnp.concatenate(
            [
                part[:, head * HEAD_DIM : (head + 1) * HEAD_DIM]
                for part in (w_key[0], w_value[0], w_query[0], out_rows)
            ],
            axis=1,
        )
        for head in range(HEADS)
    ]
    mine = jnp.where(c == 0, by_head[0], by_head[1])
    given_away = jnp.where(c == 0, by_head[1], by_head[0])
    mine, given_away, stream_f, stream_b, cot_out = lax.optimization_barrier(
        (mine, given_away, stream_f, stream_b, cot_out)
    )
    block = by_core(mine, swap(given_away, "c"))
    other_block = by_core(
        swap(mine, "yl"),
        lax.ppermute(given_away, ("yl", "c"), [(i, Y * C - 1 - i) for i in range(Y * C)]),
    )
    pair = jnp.where(y == 0, jnp.stack([block, other_block]), jnp.stack([other_block, block]))

    stream_bg = jnp.concatenate([stream_b, cot_out], axis=0)
    other_f, other_bg = swap(stream_f, "c"), swap(stream_bg, "c")
    pair, early_f, early_bg = lax.optimization_barrier((pair, stream_f, stream_bg))
    next_first = passed_along(early_f, 1)
    back_both = passed_along(early_bg, -1)

    both_f = jnp.concatenate([stream_f, other_f], axis=0)
    both_b = jnp.concatenate([stream_b, other_bg[:tokens]], axis=0)
    both_g = jnp.concatenate([cot_out, other_bg[tokens:]], axis=0)
    inverse_b, inverse_f = inverse_rms(both_b), inverse_rms(both_f)
    half_b = (both_b.astype(F32) * inverse_b).astype(BF16)
    half_f = (both_f.astype(F32) * inverse_f).astype(BF16)

    w_kvqo = lax.all_gather(pair, "z", axis=1).reshape(-1, 2 * wide)
    w_kvq, w_o = w_kvqo[:, : 3 * HEAD_DIM], w_kvqo[:, 3 * HEAD_DIM :]

    half = jnp.concatenate([half_b, half_f], axis=0)
    kv_all = dot(half, w_kvqo[:, :wide]).astype(BF16)
    kv_own = jnp.concatenate([kv_all[:chip], kv_all[chip:]], axis=1)

    def heads_together(own, other):
        return jnp.where(
            c == 0,
            jnp.concatenate([own, other], axis=1),
            jnp.concatenate([other, own], axis=1),
        )

    section = lax.axis_index("section")

    def after_first(value):
        return jnp.where(section > 0, value, jnp.zeros_like(value))[None]

    def before_last(value):
        return jnp.where(
            section < lax.axis_size("section") - 1, value, jnp.zeros_like(value)
        )[None]

    def lend(value):
        return lax.ppermute(value, "yl", [(1, 0)])

    def give_back(value):
        return lax.ppermute(value, "yl", [(0, 1)])

    order = [0] + [d for k in range(1, Z // 2) for d in (k, -k)] + [Z // 2]
    spot = jnp.arange(Z * chip, dtype=jnp.int32)
    inside = spot % chip
    inside = jnp.where(
        inside < tokens, inside + c * tokens, inside + (1 - c) * tokens - tokens
    )
    distances = jnp.asarray(np.repeat(np.array(order, np.int32), chip))
    key_index = ((y * Z + (z + distances) % Z) * chip + inside).astype(jnp.int32)
    spot = jnp.arange(2 * chip, dtype=jnp.int32)
    inside = spot % chip
    inside = jnp.where(
        inside < tokens, inside + c * tokens, inside + (1 - c) * tokens - tokens
    )
    query_index = (jnp.where(spot < chip, y, 1 - y) * Z + z) * chip + inside
    key_at, query_at = key_index[None, :], query_index[:, None]

    blocks, beside = ring_gather(
        kv_own, {2: (half, both_g), 4: (next_first, back_both)}
    )
    half_late, both_g_late = beside[2]
    next_first, back_both = beside[4]
    q_all = dot(half_late, w_kvqo[:, wide : 3 * HEAD_DIM]).astype(BF16)
    q_b, q_f = q_all[:chip], q_all[chip:]
    da_b = dot(both_g_late, w_o).astype(BF16)
    lent = lend(jnp.concatenate([q_b, da_b, q_f], axis=1))
    blocks[Z // 2], lent = lax.optimization_barrier((blocks[Z // 2], lent))
    queries_b, grads_b, queries_f = (
        jnp.concatenate([own, lent[:, k * HEAD_DIM : (k + 1) * HEAD_DIM]], axis=0)
        for k, own in enumerate((q_b, da_b, q_f))
    )
    kv = jnp.concatenate([blocks[d] for d in order], axis=0)
    def exchanged(columns):
        stats = jnp.concatenate(columns, axis=1)
        sent = jnp.where(y == 0, stats[chip:], stats[:chip])
        received = swap(sent, "yl")
        none = jnp.concatenate(
            [jnp.full((chip, 1), NEG, F32), jnp.zeros((chip, len(columns) - 1), F32)], axis=1
        )
        full = jnp.where(
            y == 0,
            jnp.concatenate([none, received], axis=0),
            jnp.concatenate([received, none], axis=0),
        )
        return [full[:, k : k + 1] for k in range(len(columns))]

    stats, out_f = kernel_call(
        statistics_kernel,
        tokens,
        [(2 * chip, 8), (2 * chip, HEAD_DIM)],
        4,
        2,
        (queries_b, grads_b, queries_f, kv, query_at, key_at),
    )
    highest, total, row_part, highest_f, total_f = (stats[:, k : k + 1] for k in range(5))
    other_highest, other_total, other_row, other_highest_f, other_total_f = exchanged(
        [highest, total, row_part, highest_f, total_f]
    )
    top, inverse, own_scale, other_scale = merged(highest, total, other_highest, other_total)
    own_scale_f = merged(highest_f, total_f, other_highest_f, other_total_f)[2]
    row_dot = row_part * own_scale + other_row * other_scale
    rows_b, kv_part = kernel_call(
        gradients_kernel,
        tokens,
        [(2 * chip, wide), (Z * chip, wide)],
        6,
        1,
        (
            queries_b,
            grads_b,
            kv,
            query_at,
            key_at,
            jnp.concatenate([top, inverse, row_dot], axis=1),
        ),
    )
    def given(rows):
        return rows[:chip] + give_back(rows[chip:].astype(BF16)).astype(F32)

    def projected(attended, received):
        return dot(attended[:tokens], w_o, 1, 1) + received.astype(F32)

    def for_other_core(attended):
        return swap(dot(attended[tokens:], w_o, 1, 1).astype(BF16), "c")

    attended_f = given(out_f * own_scale_f).astype(BF16)
    received_f = for_other_core(attended_f)
    updated = (fwd_first[0].astype(F32) + projected(attended_f, received_f)).astype(BF16)

    next_second = passed_along(updated, 1)

    own_rows = given(rows_b)
    q_grad, attended_b = own_rows[:, :HEAD_DIM].astype(BF16), own_rows[:, HEAD_DIM:].astype(BF16)
    received_b = for_other_core(attended_b)
    rec_first = (bwd_second[0].astype(F32) - projected(attended_b, received_b)).astype(BF16)

    kv_grad, beside = ring_reduce(
        {d: kv_part[i * chip : (i + 1) * chip] for i, d in enumerate(order)},
        {1: (rec_first,)},
    )
    (rec_first,) = beside[1]
    kv_grad, next_second = lax.optimization_barrier((kv_grad.astype(BF16), next_second))
    back_first = passed_along(rec_first, -1)

    grads = jnp.concatenate([kv_grad, q_grad], axis=1)
    received = swap(dot(grads[tokens:], w_kvq, 1, 1).astype(BF16), "c")
    normed_grad = dot(grads[:tokens], w_kvq, 1, 1) + received.astype(F32)
    normed_own, inverse_own = stream_b.astype(F32) * inverse_b[:tokens], inverse_b[:tokens]
    input_grad = inverse_own * (
        normed_grad - normed_own * jnp.mean(normed_grad * normed_own, axis=-1, keepdims=True)
    )
    cot_second = (grad_first[0].astype(F32) + input_grad).astype(BF16)

    zeros = jnp.zeros_like(q_grad)
    wpart = dot(
        jnp.concatenate([half_b, both_g], axis=0),
        jnp.concatenate(
            [
                jnp.concatenate([grads, zeros], axis=1),
                jnp.concatenate([zeros, zeros, zeros, attended_b], axis=1),
            ],
            axis=0,
        ),
        0,
        0,
    ).astype(BF16)
    by_chip = wpart.reshape(Y, Z, -1, 2 * wide).transpose(1, 0, 2, 3)
    over_z = lax.psum_scatter(
        by_chip.reshape(-1, 2 * wide), "z", scatter_dimension=0, tiled=True
    )
    cot_second, next_first, back_both = lax.optimization_barrier(
        (cot_second, next_first, back_both)
    )
    back_grad_second = passed_along(cot_second, -1)
    next_first = after_first(next_first)
    back_second, back_grad_first = before_last(back_both[:tokens]), before_last(back_both[tokens:])
    over_z, next_first, back_second, back_grad_first, next_second, back_first, back_grad_second = (
        lax.optimization_barrier(
            (
                over_z,
                next_first,
                back_second,
                back_grad_first,
                next_second,
                back_first,
                back_grad_second,
            )
        )
    )
    rows = over_z.shape[0] // (Y * C)
    by_owner = over_z.reshape(Y, C, rows, 2 * wide)

    def of_core(core):
        return lax.dynamic_slice(by_owner, (0, core, 0, 0), (Y, 1, rows, 2 * wide))[:, 0]

    both = jnp.concatenate([of_core(c), swap(of_core(1 - c), "c")], axis=2)
    kept = jnp.where(y == 0, both[0], both[1]).astype(F32)
    whole = kept + swap(jnp.where(y == 0, both[1], both[0]), "yl").astype(F32)
    own, other = whole[:, : 2 * wide], whole[:, 2 * wide :]

    def heads_of(index):
        span = slice(index * HEAD_DIM, (index + 1) * HEAD_DIM)
        return heads_together(own[:, span], other[:, span])

    return (
        next_first,
        after_first(next_second),
        before_last(back_first),
        back_second,
        back_grad_first,
        before_last(back_grad_second),
        heads_of(2)[None],
        heads_of(0)[None],
        heads_of(1)[None],
        heads_of(3).T[None],
    )


def solution(mesh):
    sections = mesh.devices.shape[0]
    split = Mesh(mesh.devices.reshape(sections, Y, Z, C), ("section", "yl", "z", "c"))
    fsdp = ("yl", "z", "c")
    rows = P("section", fsdp, None)
    columns = P("section", None, fsdp)
    return jax.shard_map(
        per_device,
        mesh=split,
        in_specs=(rows,) * 9 + (columns,),
        out_specs=(rows,) * 9 + (columns,),
        check_vma=False,
    )
```
